32 devices in a mesh: rows: 8 (over z, y), feat: 4 (over x, core).
Axes of the slice: x: 2, y: 2, z: 4, core: 2. Of those that a mesh axis runs over, the one named last changes fastest.
Arguments:
- targets: bfloat16 [32768, 1024], P('rows', 'feat'), may hold values from -6 to 6
- omega: bfloat16 [1024, 256], P('feat'), may hold values from -0.1875 to 0.1875
- phase: float32 [256], replicated, may hold values from -3.140625 to 3.140625
- codes: int32 [32768, 128], P('rows', 'feat'), may hold values from 0 to 31, as said below
- node: int32 [32768], P('rows'), may hold values from 0 to 7, as said below
- boot_counts: int32 [32768], P('rows'), may hold values from 0 to 3
Outputs:
- gains: float32 [1024, 31], P(('feat', 'rows'))
- best: float32 [8], replicated
The draws below stay inside these ranges and needn't reach their ends.
Inputs may be any that keep to these rules, and one draw needn't show every extreme that they name: `codes`: each feature has a lowest and a highest used bin; some features use bin 0 and some bin 32 - 1. Among the rows of each device every node holds a row with a nonzero bootstrap count.
All inputs are finite; a program needn't handle non-finite values.
Results may differ from the reference program's by a relative error of at most 0.00051.
Values may be sent and summed in bfloat16 or wider, within the bound.
No kernel may reach another device: no remote copies, remote signals or barrier semaphores. Data moves between devices by JAX's collectives and lax.ppermute only.
A program may use at most 64 MiB of HBM per device.

```python
import math
import jax
import jax.numpy as jnp
from jax import lax

F = 128
E = 1024
R = 256
BINS = 32
NODES = 8
ROWS_DEV = 4096
ROWS = 32768


def draw_codes(key, part):
    first = jax.random.fold_in(key, 11)
    second = jax.random.fold_in(key, 12)
    third = jax.random.fold_in(key, 13)
    raw = jax.random.randint(first, (ROWS, F), 0, BINS)
    feature_id = jnp.arange(F)
    lowest = jax.random.randint(second, (F,), 0, 6) * (feature_id % 4 != 0).astype(jnp.int32)
    highest = BINS - 1 - jax.random.randint(third, (F,), 0, 6) * (feature_id % 4 != 1).astype(jnp.int32)
    return jnp.clip(raw, lowest[None, :], highest[None, :]).astype(jnp.int32)


def draw_node(key, part):
    raw = jax.random.randint(jax.random.fold_in(key, 21), (ROWS,), 0, NODES)
    position = jnp.arange(ROWS) % ROWS_DEV
    return jnp.where(position < NODES, position, raw).astype(jnp.int32)


def draw_boot_counts(key, part):
    raw = jax.random.randint(jax.random.fold_in(key, 31), (ROWS,), 0, 4)
    position = jnp.arange(ROWS) % ROWS_DEV
    return jnp.where(position < NODES, jnp.maximum(raw, 1), raw).astype(jnp.int32)


def levels(stream_key, extent, pieces, low, largest):
    factor_of = 1.0
    for dim, parts in pieces:
        draws = jax.random.uniform(jax.random.fold_in(jax.random.fold_in(stream_key, 6), dim), (parts,), jnp.float32, low / len(pieces), largest / len(pieces))
        factor_of = factor_of * jnp.repeat(jnp.exp(draws), extent[dim] // parts).reshape((-1,) + (1,) * (len(extent) - 1 - dim))
    return factor_of


def gaussian(stream_key, extent, width, most, cuts=(), kind=jnp.bfloat16):
    array = jax.random.normal(stream_key, extent, jnp.float32) * width
    if len(cuts) > 0:
        array = levels(stream_key, extent, cuts, -0.22, 0.18) * array
    return jnp.clip(array, min=-most, max=most).astype(kind)


def setup_inputs(seed: int = 0) -> dict:
    key_of = jax.random.split(jax.random.key(seed), 7)
    targets = gaussian(key_of[0], (ROWS, E), 1.0, 6.0, ((0, 8), (1, 4)))
    omega = gaussian(key_of[1], (E, R), E ** -0.5, 0.1875, ((0, 4),))
    phase = jnp.clip(jax.random.uniform(key_of[2], (R,), jnp.float32, -3.140625, 3.140625), -3.140625, 3.140625)
    codes = draw_codes(jax.random.fold_in(key_of[6], 71), 0)
    node = draw_node(jax.random.fold_in(key_of[6], 71), 0)
    boot_counts = draw_boot_counts(jax.random.fold_in(key_of[6], 71), 0)
    return dict(targets=targets, omega=omega, phase=phase, codes=codes, node=node, boot_counts=boot_counts)


def split_gains(sums, tallies):
    left = jnp.cumsum(sums, axis=1)[:, :-1, :]
    whole = lax.optimization_barrier(jnp.sum(sums, axis=1))
    left_count = jnp.cumsum(tallies, axis=1)[:, :-1]
    total = lax.optimization_barrier(jnp.sum(tallies, axis=1))
    right_count = total[:, None] - left_count
    right = whole[:, None, :] - left
    differ = left / jnp.maximum(left_count, 1.0)[:, :, None] - right / jnp.maximum(right_count, 1.0)[:, :, None]
    factor = left_count * right_count / total[:, None]
    return factor * lax.optimization_barrier(jnp.sum(differ * differ, axis=2))

def reference(targets, omega, phase, codes, node, boot_counts):
    projected = jnp.dot(targets.astype(jnp.float32), omega.astype(jnp.float32), precision=lax.Precision.HIGHEST)
    fourier = (math.sqrt(2.0 / R) * jnp.cos(projected + phase[None, :])).astype(jnp.bfloat16)
    weights = boot_counts.astype(jnp.float32)
    weighted = weights[:, None] * fourier.astype(jnp.float32)
    slot_base = node * BINS

    def per_feature(column):
        index = slot_base + column
        sums = jax.ops.segment_sum(weighted, index, num_segments=NODES * BINS)
        tallies = jax.ops.segment_sum(weights, index, num_segments=NODES * BINS)
        return (sums, tallies)
    histogram, tallies = lax.map(per_feature, codes.T)
    histogram = histogram.reshape(F * NODES, BINS, R)
    tallies = tallies.reshape(F * NODES, BINS)
    gains = split_gains(histogram, tallies)
    best = lax.optimization_barrier(jnp.max(gains.reshape(F, NODES, BINS - 1), axis=(0, 2)))
    return (gains, best)
```

```python
import functools
import math

import jax
import jax.numpy as jnp
from jax import lax
from jax.experimental import pallas as pl
from jax.experimental.pallas import tpu as pltpu
from jax.sharding import PartitionSpec as P

BINS = 32
NODES = 8
LANES = 128
EXTRA = 16
STEPS = 65536.0
PARAMS = pltpu.CompilerParams(vmem_limit_bytes=40 * 1024 * 1024)
VMEM = pl.BlockSpec(memory_space=pltpu.VMEM)
SMEM = pl.BlockSpec(memory_space=pltpu.SMEM)


def rank_kernel(room, node_ref, boot_ref, pos_ref, rounds_ref):
    node = node_ref[...]
    live = boot_ref[...] > 0
    groups = node.shape[0]
    block = groups * LANES
    members = [jnp.where((node == n) & live, 1.0, 0.0) for n in range(NODES)]
    member = jnp.concatenate(members, axis=0)
    size = NODES * groups
    i = lax.broadcasted_iota(jnp.int32, (LANES, LANES), 0)
    j = lax.broadcasted_iota(jnp.int32, (LANES, LANES), 1)
    before = jnp.where(i < j, 1.0, 0.0).astype(jnp.bfloat16)
    inside = jnp.dot(member.astype(jnp.bfloat16), before, preferred_element_type=jnp.float32)
    count = jnp.sum(member, axis=1, keepdims=True)
    p = lax.broadcasted_iota(jnp.int32, (size, size), 0)
    q = lax.broadcasted_iota(jnp.int32, (size, size), 1)
    earlier = jnp.where((p // groups == q // groups) & (q < p), 1.0, 0.0).astype(jnp.bfloat16)
    spread = jnp.broadcast_to(count, (size, LANES))
    base = jnp.dot(earlier, spread.astype(jnp.bfloat16), preferred_element_type=jnp.float32)
    rank = inside + base
    pos = jnp.zeros((groups, LANES), jnp.float32)
    for n in range(NODES):
        pos += members[n] * (rank[n * groups : (n + 1) * groups] + float(n * block))
    pos_ref[...] = jnp.where(live, pos, -1.0).astype(jnp.int32)
    most = jnp.max(base + spread).astype(jnp.int32)
    rounds_ref[0] = (most + (room - 1)) // room


def sort_kernel(distance, slots, room, last, where_ref, pos_ref, t0_ref, t1_ref, o0_ref, o1_ref, codes_ref, out_ref, sorted_ref, pick):
    groups = pos_ref.shape[0]
    block = groups * LANES
    x, a, turn, rounds = where_ref[0], where_ref[1], where_ref[2], where_ref[3]
    for slot in range(slots):
        node = (x ^ distance) * slots + (a ^ slot)
        start = node * block + turn * room
        wanted = start + lax.broadcasted_iota(jnp.int32, (room, LANES), 0)
        for g in range(groups):
            pick[slot * room : (slot + 1) * room, g * LANES : (g + 1) * LANES] = jnp.where(
                pos_ref[g : g + 1, :] == wanted, 1.0, 0.0
            ).astype(jnp.bfloat16)
    s0 = jnp.dot(pick[...], t0_ref[...], preferred_element_type=jnp.float32).astype(jnp.bfloat16)
    s1 = jnp.dot(pick[...], t1_ref[...], preferred_element_type=jnp.float32).astype(jnp.bfloat16)
    partial = jnp.dot(s0, o0_ref[...], preferred_element_type=jnp.float32)
    partial += jnp.dot(s1, o1_ref[...], preferred_element_type=jnp.float32)
    turns = partial * (0.5 / math.pi)
    turns = turns - jnp.floor(turns)
    if distance:
        coded = jnp.minimum((turns * STEPS).astype(jnp.int32), 65535) - 32768
        out_ref[...] = coded.astype(jnp.int16)
    else:
        out_ref[...] = turns
    moved = lax.dot_general(
        codes_ref[...], pick[...], (((1,), (1,)), ((), ())), preferred_element_type=jnp.float32
    )
    line = lax.broadcasted_iota(jnp.int32, moved.shape, 0)
    moved = jnp.where(line == last, rounds.astype(jnp.float32), moved)
    sorted_ref[...] = moved.astype(jnp.bfloat16)


def cosine_kernel(slots, own_ref, phase_ref, *refs):
    received, outs = refs[:-slots], refs[-slots:]
    width = phase_ref.shape[1]
    room = outs[0].shape[0]
    scaling = math.sqrt(2.0 / width)
    series = [(-1.0) ** (k + 1) * (2 * math.pi) ** (2 * k + 1) / math.factorial(2 * k + 1) for k in range(7)]
    shift = phase_ref[...] * (0.5 / math.pi)
    for slot in range(slots):
        rows = pl.ds(slot * room, room)
        turns = own_ref[rows, :] + shift
        for ref in received:
            turns += (ref[rows, :].astype(jnp.float32) + 32768.5) * (1.0 / STEPS)
        turns = jnp.abs(turns - jnp.floor(turns + 0.5)) - 0.25
        square = turns * turns
        value = jnp.full_like(turns, series[-1])
        for term in series[-2::-1]:
            value = value * square + term
        outs[slot][...] = (scaling * (value * turns)).astype(jnp.bfloat16)


def gains_of(left, counts):
    whole = left[..., BINS - 1 :, :]
    total = counts[..., BINS - 1 :, :]
    other = total - counts
    differ = left * (1.0 / jnp.maximum(counts, 1.0)) - (whole - left) * (1.0 / jnp.maximum(other, 1.0))
    return (counts * other / total) * jnp.sum(differ * differ, axis=-1, keepdims=True)


def histogram_kernel(features, codes_ref, *refs):
    *pieces, left_ref, counts_ref, gains_ref, table = refs
    length = pieces[0].shape[0]
    slots = features * BINS
    threshold = lax.broadcasted_iota(jnp.int32, (BINS, length), 0).astype(jnp.float32)
    for index, piece in enumerate(pieces):
        span = slice(index * length, (index + 1) * length)
        codes = codes_ref[:, span].astype(jnp.float32)
        weight = codes[features : features + 1, :]
        for f in range(features):
            rows = slice(f * BINS, (f + 1) * BINS)
            entry = jnp.where(codes[f : f + 1, :] <= threshold, weight, 0.0)
            table[rows, :] = entry.astype(jnp.bfloat16)
            folded = entry[:, :LANES]
            for g in range(1, length // LANES):
                folded += entry[:, g * LANES : (g + 1) * LANES]
            if index:
                folded += counts_ref[rows, :]
            counts_ref[rows, :] = folded
        sums = jnp.dot(table[...], piece[...], preferred_element_type=jnp.float32)
        if index:
            left_ref[...] += sums
        else:
            left_ref[...] = sums
    per_line = LANES // BINS
    i = lax.broadcasted_iota(jnp.int32, (LANES, LANES), 0)
    j = lax.broadcasted_iota(jnp.int32, (LANES, LANES), 1)
    for line in range(slots // LANES):
        columns = []
        for f in range(line * per_line, (line + 1) * per_line):
            rows = slice(f * BINS, (f + 1) * BINS)
            counts = jnp.sum(counts_ref[rows, :], axis=1, keepdims=True)
            columns.append(gains_of(left_ref[rows, :], counts))
        column = jnp.concatenate(columns, axis=0)
        gains_ref[line : line + 1, :] = jnp.sum(jnp.where(i == j, column, 0.0), axis=0, keepdims=True)


def split_rows(mesh_sizes, targets, omega, phase, codes, node, boot_counts):
    groups_all, feat_all = mesh_sizes
    chips = feat_all // 2
    slots = NODES // chips
    copies = groups_all // slots
    rows_dev, feat_dev = codes.shape
    width = omega.shape[1]
    block = rows_dev // 2
    room = block // NODES
    owned = feat_dev * NODES // groups_all
    per_owner = max(1, owned // NODES)
    sets = feat_dev // per_owner
    lines = sets // copies
    part = lines * per_owner
    features = chips * part

    feat, place = lax.axis_index("feat"), lax.axis_index("rows")
    x, core = feat // 2, feat % 2
    major, minor = place // copies, place % copies

    def permute(axis, size, distance, array):
        return lax.ppermute(array, axis, [(i, i ^ distance) for i in range(size)])

    swap = functools.partial(permute, "feat", feat_all, 1)

    def along_x(distance, array):
        return permute("feat", feat_all, 2 * distance, array)

    def along_major(distance, array):
        return permute("rows", groups_all, copies * distance, array)

    def along_minor(distance, array):
        return permute("rows", groups_all, distance, array)

    mine, theirs = core * block, (1 - core) * block
    targets_theirs = swap(lax.dynamic_slice_in_dim(targets, theirs, block, 0))
    targets_mine = lax.dynamic_slice_in_dim(targets, mine, block, 0)
    omega_theirs = swap(omega)

    half = codes.astype(jnp.bfloat16).T.reshape(lines, copies, per_owner, rows_dev)
    half = jnp.concatenate([lax.dynamic_slice_in_dim(half, minor ^ d, 1, 1) for d in range(copies)], axis=1)
    half = half.transpose(1, 0, 2, 3).reshape(feat_dev, rows_dev)
    half_mine = lax.dynamic_slice_in_dim(half, mine, block, 1)
    half_theirs = swap(lax.dynamic_slice_in_dim(half, theirs, block, 1))
    node_mine = lax.dynamic_slice_in_dim(node, mine, block, 0).reshape(block // LANES, LANES)
    boot_mine = lax.dynamic_slice_in_dim(boot_counts, mine, block, 0).reshape(block // LANES, LANES)
    weights = boot_mine.astype(jnp.bfloat16).reshape(1, block)
    extra = jnp.concatenate([weights, jnp.zeros((EXTRA - 1, block), jnp.bfloat16)], axis=0)
    table = jnp.concatenate([half_mine, half_theirs, extra], axis=0)
    both = 2 * feat_dev

    pos, rounds = pl.pallas_call(
        functools.partial(rank_kernel, room),
        out_shape=(
            jax.ShapeDtypeStruct((block // LANES, LANES), jnp.int32),
            jax.ShapeDtypeStruct((1,), jnp.int32),
        ),
        in_specs=[VMEM, VMEM],
        out_specs=(VMEM, SMEM),
        compiler_params=PARAMS,
        name="rank",
    )(node_mine, boot_mine)

    def sort(distance, turn):
        return pl.pallas_call(
            functools.partial(sort_kernel, distance, slots, room, both + 1),
            out_shape=(
                jax.ShapeDtypeStruct((slots * room, width), jnp.int16 if distance else jnp.float32),
                jax.ShapeDtypeStruct((both + EXTRA, slots * room), jnp.bfloat16),
            ),
            in_specs=[SMEM] + [VMEM] * 6,
            out_specs=(VMEM, VMEM),
            scratch_shapes=[pltpu.VMEM((slots * room, block), jnp.bfloat16)],
            compiler_params=PARAMS,
            cost_estimate=pl.CostEstimate(
                flops=2 * slots * room * block * (2 * targets.shape[1] + both), bytes_accessed=4 << 20, transcendentals=0
            ),
            name="sort",
        )(
            jnp.stack([x, major, turn, rounds[0]]).astype(jnp.int32),
            pos, targets_mine, targets_theirs, omega, omega_theirs, table,
        )

    def one_round(turn):
        sent = [sort(d, turn) for d in range(1, chips)]
        angles = [along_x(d, sent[d - 1][0]) for d in range(1, chips)]
        own_angles, own_codes = sort(0, turn)
        chip_codes = [own_codes] + [along_x(d, sent[d - 1][1][:both]) for d in range(1, chips)]
        chip_codes = jnp.concatenate(chip_codes, axis=0)
        arrived = []
        for d in range(slots):
            piece = chip_codes[:, d * room : (d + 1) * room]
            arrived.append(along_major(d, piece) if d else piece)
        node_codes = jnp.concatenate(arrived, axis=1)
        span = slots * room

        fourier = pl.pallas_call(
            functools.partial(cosine_kernel, slots),
            out_shape=tuple(jax.ShapeDtypeStruct((room, width), jnp.bfloat16) for _ in range(slots)),
            in_specs=[VMEM] * (chips + 1),
            out_specs=tuple(VMEM for _ in range(slots)),
            compiler_params=PARAMS,
            cost_estimate=pl.CostEstimate(flops=30 * span * width, bytes_accessed=2 << 20, transcendentals=0),
            name="cosine",
        )(own_angles, phase.reshape(1, width), *angles)
        fourier = jnp.concatenate([along_major(d, fourier[d]) if d else fourier[d] for d in range(slots)], axis=0)

        first, rest = node_codes[:both], node_codes[both + EXTRA :]
        extras = node_codes[both : both + EXTRA]
        by_part = jnp.concatenate([first, rest], axis=0).reshape(chips, 2, copies, part, span)
        held = []
        for d in range(copies):
            piece = jnp.concatenate([by_part[:, :, d].reshape(chips * 2 * part, span), extras], axis=0)
            held.append(along_minor(d, piece) if d else piece)
        held = jnp.concatenate(held, axis=1)
        by_core = held[: 2 * features].reshape(chips, 2, part, copies * span)
        keep = jnp.concatenate([by_core[:, 0].reshape(features, copies * span), held[2 * features :]], axis=0)
        give = jnp.concatenate([by_core[:, 1].reshape(features, copies * span), held[2 * features :]], axis=0)
        final_codes = jnp.concatenate([keep, swap(give)], axis=1)

        pieces = [along_minor(d, fourier) if d else fourier for d in range(copies)]
        pieces = pieces + [swap(piece) for piece in pieces]
        left, counts, gains = pl.pallas_call(
            functools.partial(histogram_kernel, features),
            out_shape=(
                jax.ShapeDtypeStruct((features * BINS, width), jnp.float32),
                jax.ShapeDtypeStruct((features * BINS, LANES), jnp.float32),
                jax.ShapeDtypeStruct((features * BINS // LANES, LANES), jnp.float32),
            ),
            in_specs=[VMEM] * (1 + len(pieces)),
            out_specs=(VMEM, VMEM, VMEM),
            scratch_shapes=[pltpu.VMEM((features * BINS, span), jnp.bfloat16)],
            compiler_params=PARAMS,
            name="histogram",
        )(final_codes, *pieces)
        return left, counts, gains, final_codes[features + 1]

    left, counts, gains, flags = one_round(jnp.int32(0))
    needed = jnp.max(flags.astype(jnp.float32)).astype(jnp.int32)

    def more_rounds():
        def step(state):
            turn, left, counts = state
            more_left, more_counts, _, _ = one_round(turn)
            return turn + 1, left + more_left, counts + more_counts

        _, all_left, all_counts = lax.while_loop(lambda state: state[0] < needed, step, (jnp.int32(1), left, counts))
        tallies = jnp.sum(all_counts, axis=1).reshape(features, BINS, 1)
        return gains_of(all_left.reshape(features, BINS, width), tallies).reshape(gains.shape)

    gains = lax.cond(needed > 1, more_rounds, lambda: gains)
    gains = gains.reshape(chips, lines, per_owner, BINS)
    largest = jnp.max(gains[..., : BINS - 1])
    gains = lax.switch(x, [functools.partial(lambda g, o: jnp.stack([g[i ^ o] for i in range(chips)]), gains, o) for o in range(chips)])

    line_of = [(i // (groups_all // sets)) // copies for i in range(groups_all)]
    load = per_owner * BINS
    send = jnp.stack([gains[:, line].reshape(chips, 1, load) for line in line_of])
    send = jnp.broadcast_to(send, (groups_all, chips, 2, load))
    top = jnp.full((groups_all, chips, 2, load), largest)
    send = jnp.stack([send, top], axis=3).reshape(groups_all * feat_all, 2, load)
    got = lax.all_to_all(send, ("rows", "feat"), 0, 0).reshape(slots, copies, chips, 2, 2, load)
    best = jnp.max(got[:, :, :, :, 1, 0], axis=(1, 3)).T.reshape(NODES)
    source = (place // (groups_all // sets)) % copies
    took = lax.dynamic_slice_in_dim(got[:, :, :, :, 0], source, 1, 1)
    took = lax.dynamic_slice_in_dim(took, core, 1, 3)
    took = took.reshape(slots, chips, per_owner, BINS).transpose(2, 1, 0, 3).reshape(per_owner * NODES, BINS)
    took = lax.dynamic_slice_in_dim(took, (place * owned) % (per_owner * NODES), owned, 0)
    return took[:, : BINS - 1], best


def solution(mesh):
    in_specs = (P("rows", "feat"), P("feat", None), P(), P("rows", "feat"), P("rows"), P("rows"))
    out_specs = (P(("feat", "rows"), None), P())
    sizes = (mesh.shape["rows"], mesh.shape["feat"])
    return jax.shard_map(
        functools.partial(split_rows, sizes), mesh=mesh, in_specs=in_specs, out_specs=out_specs, check_vma=False
    )
```

```python
import functools
import math

import jax
import jax.numpy as jnp
from jax import lax
from jax.experimental import pallas as pl
from jax.experimental.pallas import tpu as pltpu
from jax.sharding import PartitionSpec as P

BINS = 32
NODES = 8
LANES = 128
EXTRA = 16
STEPS = 65536.0
PARAMS = pltpu.CompilerParams(vmem_limit_bytes=32 * 1024 * 1024)
VMEM = pl.BlockSpec(memory_space=pltpu.VMEM)
SMEM = pl.BlockSpec(memory_space=pltpu.SMEM)


def rank_of(node, live):
    groups = node.shape[0]
    block = groups * LANES
    members = [jnp.where((node == n) & live, 1.0, 0.0) for n in range(NODES)]
    member = jnp.concatenate(members, axis=0)
    size = NODES * groups
    i = lax.broadcasted_iota(jnp.int32, (LANES, LANES), 0)
    j = lax.broadcasted_iota(jnp.int32, (LANES, LANES), 1)
    before = jnp.where(i < j, 1.0, 0.0).astype(jnp.bfloat16)
    inside = jnp.dot(member.astype(jnp.bfloat16), before, preferred_element_type=jnp.float32)
    count = jnp.sum(member, axis=1, keepdims=True)
    p = lax.broadcasted_iota(jnp.int32, (size, size), 0)
    q = lax.broadcasted_iota(jnp.int32, (size, size), 1)
    earlier = jnp.where((p // groups == q // groups) & (q < p), 1.0, 0.0).astype(jnp.bfloat16)
    spread = jnp.broadcast_to(count, (size, LANES))
    base = jnp.dot(earlier, spread.astype(jnp.bfloat16), preferred_element_type=jnp.float32)
    rank = inside + base
    pos = jnp.zeros((groups, LANES), jnp.float32)
    for n in range(NODES):
        pos += members[n] * (rank[n * groups : (n + 1) * groups] + float(n * block))
    return jnp.where(live, pos, -1.0).astype(jnp.int32), jnp.max(base + spread).astype(jnp.int32)


def choose_rows(pos_ref, pick, distance, slots, room, x, a, turn):
    groups = pos_ref.shape[0]
    block = groups * LANES
    for slot in range(slots):
        node = (x ^ distance) * slots + (a ^ slot)
        start = node * block + turn * room
        wanted = start + lax.broadcasted_iota(jnp.int32, (room, LANES), 0)
        for g in range(groups):
            pick[slot * room : (slot + 1) * room, g * LANES : (g + 1) * LANES] = jnp.where(
                pos_ref[g : g + 1, :] == wanted, 1.0, 0.0
            ).astype(jnp.bfloat16)


def moved(codes, pick):
    return lax.dot_general(codes, pick, (((1,), (1,)), ((), ())), preferred_element_type=jnp.float32)


def theirs_kernel(targets_ref, theirs_ref, sem):
    block = theirs_ref.shape[0]
    first = pl.multiple_of((1 - (lax.axis_index("feat") & 1)) * block, block)
    copy = pltpu.make_async_copy(targets_ref.at[pl.ds(first, block), :], theirs_ref, sem)
    copy.start()
    copy.wait()


def prepare_kernel(copies, codes_ref, boot_ref, give_ref, mine_ref):
    block = mine_ref.shape[1]
    features = codes_ref.shape[0]
    part = features // copies
    core = lax.axis_index("feat") & 1
    minor = lax.axis_index("rows") & (copies - 1)
    mine, theirs = pl.multiple_of(core * block, block), pl.multiple_of((1 - core) * block, block)
    for out_ref, first in ((give_ref, theirs), (mine_ref, mine)):
        parts = [codes_ref[pl.ds((minor ^ d) * part, part), pl.ds(first, block)] for d in range(copies)]
        out_ref[:features, :] = jnp.concatenate(parts, axis=0).astype(jnp.float32).astype(jnp.bfloat16)
    mine_ref[features:, :] = jnp.zeros((EXTRA, block), jnp.bfloat16)
    first = pl.multiple_of(core * (block // LANES), block // LANES)
    weights = boot_ref[pl.ds(first, block // LANES), :].astype(jnp.float32)
    line = lax.broadcasted_iota(jnp.int32, (EXTRA, LANES), 0)
    for g in range(block // LANES):
        row = jnp.where(line == 0, weights[g : g + 1, :], 0.0)
        mine_ref[features:, g * LANES : (g + 1) * LANES] = row.astype(jnp.bfloat16)


def order_kernel(chips, slots, room, turn_ref, node_ref, boot_ref, mine_ref, taken_ref, pos_ref, rounds_ref, *outs):
    feat, place = lax.axis_index("feat"), lax.axis_index("rows")
    groups = pos_ref.shape[0]
    first = pl.multiple_of((feat & 1) * groups, groups)
    pos, most = rank_of(node_ref[pl.ds(first, groups), :], boot_ref[pl.ds(first, groups), :] > 0)
    pos_ref[...] = pos
    rounds_ref[0] = (most + (room - 1)) // room
    features = taken_ref.shape[0]
    codes = jnp.concatenate([mine_ref[:features, :], taken_ref[...]], axis=0)
    for distance in range(1, chips):
        pick, sorted_ref = outs[2 * distance - 2 : 2 * distance]
        choose_rows(pos_ref, pick, distance, slots, room, feat >> 1, major_of(place, slots), turn_ref[0])
        sorted_ref[...] = moved(codes, pick[...]).astype(jnp.bfloat16)


def major_of(place, slots):
    copies = lax.axis_size("rows") // slots
    return place >> (copies.bit_length() - 1)


def turns_of(pick, targets_ref, t0, t1_ref, o0_ref, o1_ref, sem):
    block = t0.shape[0]
    first = pl.multiple_of((lax.axis_index("feat") & 1) * block, block)
    copy = pltpu.make_async_copy(targets_ref.at[pl.ds(first, block), :], t0, sem)
    copy.start()
    s1 = jnp.dot(pick[...], t1_ref[...], preferred_element_type=jnp.float32).astype(jnp.bfloat16)
    partial = jnp.dot(s1, o1_ref[...], preferred_element_type=jnp.float32)
    copy.wait()
    s0 = jnp.dot(pick[...], t0[...], preferred_element_type=jnp.float32).astype(jnp.bfloat16)
    partial += jnp.dot(s0, o0_ref[...], preferred_element_type=jnp.float32)
    turns = partial * (0.5 / math.pi)
    return turns - jnp.floor(turns)


def send_kernel(rounds_ref, pick_ref, targets_ref, t1_ref, o0_ref, o1_ref, *refs):
    outs, (passed_ref, t0, sem) = refs[:-3], refs[-3:]
    passed_ref[0] = rounds_ref[0]
    turns = turns_of(pick_ref, targets_ref, t0, t1_ref, o0_ref, o1_ref, sem)
    coded = (jnp.minimum((turns * STEPS).astype(jnp.int32), 65535) - 32768).astype(jnp.int16)
    first = 0
    for out_ref in outs:
        out_ref[...] = coded[first : first + out_ref.shape[0]]
        first += out_ref.shape[0]


def codes_kernel(chips, slots, room, turn_ref, rounds_ref, pos_ref, mine_ref, taken_ref, *refs):
    received, pick, pieces = refs[: chips - 1], refs[chips - 1], refs[chips:]
    feat, place = lax.axis_index("feat"), lax.axis_index("rows")
    choose_rows(pos_ref, pick, 0, slots, room, feat >> 1, major_of(place, slots), turn_ref[0])
    features = taken_ref.shape[0]
    both = 2 * features
    codes = jnp.concatenate([mine_ref[:features, :], taken_ref[...], mine_ref[features:, :]], axis=0)
    own = moved(codes, pick[...])
    line = lax.broadcasted_iota(jnp.int32, own.shape, 0)
    own = jnp.where(line == both + 1, rounds_ref[0].astype(jnp.float32), own).astype(jnp.bfloat16)
    for slot in range(slots):
        span = slice(slot * room, (slot + 1) * room)
        pieces[slot][: both + EXTRA, :] = own[:, span]
        for d in range(1, chips):
            first = both * d + EXTRA
            pieces[slot][first : first + both, :] = received[d - 1][:, span]


def keep_kernel(pick_ref, targets_ref, t1_ref, o0_ref, o1_ref, out_ref, t0, sem):
    out_ref[...] = turns_of(pick_ref, targets_ref, t0, t1_ref, o0_ref, o1_ref, sem)


def cosine_kernel(chips, first, own_ref, phase_ref, *refs):
    received, outs = refs[: chips - 1], refs[chips - 1 :]
    width = phase_ref.shape[1]
    room = outs[0].shape[0]
    scaling = math.sqrt(2.0 / width)
    series = [(-1.0) ** (k + 1) * (2 * math.pi) ** (2 * k + 1) / math.factorial(2 * k + 1) for k in range(7)]
    shift = phase_ref[...] * (0.5 / math.pi)
    for slot, out_ref in enumerate(outs):
        turns = own_ref[(first + slot) * room : (first + slot + 1) * room, :] + shift
        for ref in received:
            turns += (ref[slot * room : (slot + 1) * room, :].astype(jnp.float32) + 32768.5) * (1.0 / STEPS)
        turns = jnp.abs(turns - jnp.floor(turns + 0.5)) - 0.25
        square = turns * turns
        value = jnp.full_like(turns, series[-1])
        for term in series[-2::-1]:
            value = value * square + term
        out_ref[...] = (scaling * (value * turns)).astype(jnp.bfloat16)


def far_cosine_kernel(chips, first, slots, own_ref, phase_ref, *refs):
    split = chips - 1 + slots
    pieces, codes_ref = refs[chips - 1 : split], refs[-1]
    cosine_kernel(chips, first, own_ref, phase_ref, *refs[: chips - 1], *refs[split:-1])
    room = pieces[0].shape[1]
    for slot, piece in enumerate(pieces):
        codes_ref[:, slot * room : (slot + 1) * room] = piece[...]


def gains_of(left, counts):
    whole = left[..., BINS - 1 :, :]
    total = counts[..., BINS - 1 :, :]
    other = total - counts
    differ = left * (1.0 / jnp.maximum(counts, 1.0)) - (whole - left) * (1.0 / jnp.maximum(other, 1.0))
    return (counts * other / total) * jnp.sum(differ * differ, axis=-1, keepdims=True)


def add_rows(features, offset, weight_at, codes_ref, pieces, table, left_ref, counts_ref, fresh):
    room = pieces[0].shape[0]
    length = room * len(pieces)
    threshold = lax.broadcasted_iota(jnp.int32, (BINS, length), 0).astype(jnp.float32)
    codes = codes_ref[...].astype(jnp.float32)
    weight = codes[weight_at : weight_at + 1, :]
    for f in range(features):
        rows = slice(f * BINS, (f + 1) * BINS)
        entry = jnp.where(codes[offset + f : offset + f + 1, :] <= threshold, weight, 0.0)
        table[rows, :] = entry.astype(jnp.bfloat16)
        folded = entry[:, :LANES]
        for g in range(1, length // LANES):
            folded += entry[:, g * LANES : (g + 1) * LANES]
        counts_ref[rows, :] = folded if fresh else counts_ref[rows, :] + folded
    block = jnp.concatenate([piece[...] for piece in pieces], axis=0)
    sums = jnp.dot(table[...], block, preferred_element_type=jnp.float32)
    left_ref[...] = sums if fresh else left_ref[...] + sums


def sums_kernel(features, first, copies, *refs):
    sides, pieces, earlier = refs[: 2 * copies], refs[2 * copies : 4 * copies], refs[4 * copies : -3]
    left_ref, counts_ref, table = refs[-3:]
    add_rows(features, first, sides, pieces, earlier, left_ref, counts_ref, table)


def add_rows(features, first, sides, pieces, earlier, left_ref, counts_ref, table):
    rows = pieces[0].shape[0]
    span = slice(first, first + rows)
    length = rows * len(pieces)
    threshold = lax.broadcasted_iota(jnp.int32, (BINS, length), 0).astype(jnp.float32)
    codes, weights = [], []
    for index, side in enumerate(sides):
        lines = side[:, span].astype(jnp.float32)
        codes_at, weight_at = (EXTRA, 0) if index % 2 else (0, features)
        codes.append(lines[codes_at : codes_at + features])
        weights.append(lines[weight_at : weight_at + 1])
    codes, weight = jnp.concatenate(codes, axis=1), jnp.concatenate(weights, axis=1)
    for f in range(features):
        rows = slice(f * BINS, (f + 1) * BINS)
        entry = jnp.where(codes[f : f + 1, :] <= threshold, weight, 0.0)
        table[rows, :] = entry.astype(jnp.bfloat16)
        folded = entry[:, :LANES]
        for g in range(1, length // LANES):
            folded += entry[:, g * LANES : (g + 1) * LANES]
        counts_ref[rows, :] = earlier[1][rows, :] + folded if earlier else folded
    block = jnp.concatenate([piece[...] for piece in pieces], axis=0)
    sums = jnp.dot(table[...], block, preferred_element_type=jnp.float32)
    left_ref[...] = earlier[0][...] + sums if earlier else sums


def gains_kernel(features, first, copies, lines, sets, groups, chips, *refs):
    sides, pieces, earlier = refs[: 2 * copies], refs[2 * copies : 4 * copies], refs[4 * copies : -5]
    left_ref, counts_ref, send_ref, needed_ref, table = refs[-5:]
    add_rows(features, first, sides, pieces, earlier, left_ref, counts_ref, table)
    needed = 0.0
    for index, side in enumerate(sides):
        flags_at = 0 if index % 2 else features
        flags = side[flags_at : flags_at + EXTRA, :].astype(jnp.float32)
        line = lax.broadcasted_iota(jnp.int32, flags.shape, 0)
        needed = jnp.maximum(needed, jnp.max(jnp.where(line == 1, flags, 0.0)))
    needed_ref[0] = needed.astype(jnp.int32)
    x = lax.axis_index("feat") >> 1
    columns = []
    largest = jnp.zeros((1, 1), jnp.float32)
    threshold = lax.broadcasted_iota(jnp.int32, (BINS, 1), 0)
    for f in range(features):
        rows = slice(f * BINS, (f + 1) * BINS)
        counts = jnp.sum(counts_ref[rows, :], axis=1, keepdims=True)
        column = gains_of(left_ref[rows, :], counts)
        column = jnp.where(threshold < BINS - 1, column, 0.0)
        largest = jnp.maximum(largest, jnp.max(column, axis=0, keepdims=True))
        columns.append(column)
    load = send_ref.shape[2]
    wide = load // BINS
    fill = jnp.broadcast_to(largest, (BINS, 1))
    i = lax.broadcasted_iota(jnp.int32, (load, load), 0)
    j = lax.broadcasted_iota(jnp.int32, (load, load), 1)
    for d in range(chips):
        for line in range(lines):
            first = (d * lines + line) * wide
            column = jnp.concatenate([jnp.where(threshold < BINS - 1, c, fill) for c in columns[first : first + wide]], axis=0)
            row = jnp.sum(jnp.where(i == j, column, 0.0), axis=0, keepdims=True)
            for place in range(groups):
                if place // (groups // sets) % lines == line:
                    for core in range(2):
                        send_ref[place * 2 * chips + 2 * (x ^ d) + core] = row


def finish_kernel(chips, slots, copies, lines, sets, groups, got_ref, gains_ref, best_ref, rows_ref):
    feat, place = lax.axis_index("feat"), lax.axis_index("rows")
    core = feat & 1
    per_set = groups // sets
    source = (place >> (per_set.bit_length() - 1)) >> (lines.bit_length() - 1)
    load = got_ref.shape[2]
    own, top = [], []
    for node in range(NODES):
        x, a = node // slots, node % slots
        index = lambda b, c: (a * copies + b) * 2 * chips + 2 * x + c
        own.append(got_ref[index(source, core)])
        largest = got_ref[index(0, 0)]
        for b in range(copies):
            for c in range(2):
                largest = jnp.maximum(largest, got_ref[index(b, c)])
        top.append(largest)
    own, top = jnp.concatenate(own, axis=0), jnp.concatenate(top, axis=0)
    for f in range(load // BINS):
        rows_ref[f * NODES : (f + 1) * NODES, :] = own[:, f * BINS : (f + 1) * BINS - 1]
    owned = gains_ref.shape[0]
    first = (place * owned) & (rows_ref.shape[0] - 1)
    gains_ref[...] = rows_ref[pl.ds(first, owned), :]
    i = lax.broadcasted_iota(jnp.int32, (NODES, NODES), 0)
    j = lax.broadcasted_iota(jnp.int32, (NODES, NODES), 1)
    best_ref[...] = jnp.sum(jnp.where(i == j, top[:, BINS - 1 : BINS], 0.0), axis=0, keepdims=True)


def split_rows(mesh_sizes, targets, omega, phase, codes, node, boot_counts):
    groups_all, feat_all = mesh_sizes
    chips = feat_all // 2
    slots = NODES // chips
    copies = groups_all // slots
    rows_dev, feat_dev = codes.shape
    width = omega.shape[1]
    block = rows_dev // 2
    room = block // NODES
    owned = feat_dev * NODES // groups_all
    per_owner = max(1, owned // NODES)
    sets = feat_dev // per_owner
    lines = sets // copies
    part = lines * per_owner
    features = chips * part

    feat = lax.axis_index("feat")
    x = feat // 2
    both = 2 * feat_dev
    span = slots * room
    load = per_owner * BINS
    columns = targets.shape[1]

    def permute(axis, size, distance, array):
        return lax.ppermute(array, axis, [(i, i ^ distance) for i in range(size)])

    swap = functools.partial(permute, "feat", feat_all, 1)

    def along_x(distance, array):
        return permute("feat", feat_all, 2 * distance, array)

    def along_major(distance, array):
        return permute("rows", groups_all, copies * distance, array)

    def along_minor(distance, array):
        return permute("rows", groups_all, distance, array)

    def shaped(kind, *shape):
        return jax.ShapeDtypeStruct(shape, kind)

    def kernel(body, name, outs, scratch=(), micros=0.0, **more):
        def call(*arrays):
            ins = [SMEM if a.shape == (1,) else pl.BlockSpec(memory_space=pl.ANY) if a is targets else VMEM for a in arrays]
            return pl.pallas_call(
                body, out_shape=tuple(outs), in_specs=ins, scratch_shapes=list(scratch), compiler_params=PARAMS, name=name,
                out_specs=tuple(SMEM if out.shape == (1,) else VMEM for out in outs),
                cost_estimate=pl.CostEstimate(flops=int(micros * 1e9), bytes_accessed=1 << 16, transcendentals=0), **more,
            )(*arrays)

        return call

    half_targets = [pltpu.VMEM((block, columns), jnp.bfloat16), pltpu.SemaphoreType.DMA(())]
    first_round = jnp.zeros((1,), jnp.int32)
    node_lines = node.reshape(rows_dev // LANES, LANES)
    boot_lines = boot_counts.reshape(rows_dev // LANES, LANES)
    (theirs,) = kernel(
        theirs_kernel, "theirs", [shaped(jnp.bfloat16, block, columns)], [pltpu.SemaphoreType.DMA(())]
    )(targets)
    theirs = swap(theirs)
    give, mine = kernel(
        functools.partial(prepare_kernel, copies), "prepare",
        [shaped(jnp.bfloat16, feat_dev, block), shaped(jnp.bfloat16, feat_dev + EXTRA, block)], micros=1.0,
    )(codes.T, boot_lines)
    taken, omega_theirs = swap(give), swap(omega)
    near = slots // 2
    parts = [near, slots - near]

    def one_round(turn):
        outs = [shaped(jnp.int32, block // LANES, LANES), shaped(jnp.int32, 1)]
        for d in range(1, chips):
            outs += [shaped(jnp.bfloat16, span, block), shaped(jnp.bfloat16, both, span)]
        pos, rounds, *chosen = kernel(functools.partial(order_kernel, chips, slots, room), "order", outs, micros=3.0)(
            turn, node_lines, boot_lines, mine, taken
        )
        chip_codes = [along_x(d, chosen[2 * d - 1]) for d in range(1, chips)]
        angles = []
        for d in range(1, chips):
            outs = [shaped(jnp.int16, n * room, width) for n in parts] + [shaped(jnp.int32, 1)]
            *sent, rounds = kernel(send_kernel, "send", outs, half_targets, 4.0)(
                rounds, chosen[2 * d - 2], targets, theirs, omega, omega_theirs
            )
            angles.append([along_x(d, s) for s in sent])
        pick, *pieces = kernel(
            functools.partial(codes_kernel, chips, slots, room), "codes",
            [shaped(jnp.bfloat16, span, block)] + [shaped(jnp.bfloat16, chips * both + EXTRA, room)] * slots, micros=3.0,
        )(turn, rounds, pos, mine, taken, *chip_codes)
        pieces = [along_major(d, pieces[d]) if d else pieces[d] for d in range(slots)]
        (own_angles,) = kernel(keep_kernel, "keep", [shaped(jnp.float32, span, width)], half_targets, 4.0)(
            pick, targets, theirs, omega, omega_theirs
        )
        line = phase.reshape(1, width)
        *far, node_codes = kernel(
            functools.partial(far_cosine_kernel, chips, near, slots), "cosine",
            [shaped(jnp.bfloat16, room, width)] * parts[1] + [shaped(jnp.bfloat16, chips * both + EXTRA, span)], micros=1.0,
        )(own_angles, line, *[a[1] for a in angles], *pieces)
        far = [along_major(near + i, f) for i, f in enumerate(far)]
        close = kernel(
            functools.partial(cosine_kernel, chips, 0), "cosine", [shaped(jnp.bfloat16, room, width)] * near, micros=1.0
        )(own_angles, line, *[a[0] for a in angles])
        close = [along_major(d, f) if d else f for d, f in enumerate(close)]

        extras = node_codes[both : both + EXTRA]
        by_part = jnp.concatenate([node_codes[:both], node_codes[both + EXTRA :]], axis=0)
        by_part = by_part.reshape(chips, 2, copies, part, span)
        sides = []
        for d in range(copies):
            nearer = by_part[:, 0, d].reshape(features, span)
            farther = by_part[:, 1, d].reshape(features, span)
            held = jnp.concatenate([nearer, extras, farther], axis=0)
            held = along_minor(d, held) if d else held
            sides += [held[: features + EXTRA], swap(held[features:])]
        sums = [shaped(jnp.float32, features * BINS, width), shaped(jnp.float32, features * BINS, LANES)]
        state = ()
        for part_of, first in ((close, 0), (far, near * room)):
            mine_here = jnp.concatenate(part_of, axis=0)
            rows = []
            for d in range(copies):
                here = along_minor(d, mine_here) if d else mine_here
                rows += [here, swap(here)]
            last = part_of is far
            if last:
                body = functools.partial(gains_kernel, features, first, copies, lines, sets, groups_all, chips)
                outs = sums + [shaped(jnp.float32, groups_all * feat_all, 1, load), shaped(jnp.int32, 1)]
            else:
                body, outs = functools.partial(sums_kernel, features, first, copies), sums
            at = len(sides) + len(rows)
            scratch = [pltpu.VMEM((features * BINS, 2 * copies * mine_here.shape[0]), jnp.bfloat16)]
            state = kernel(
                body, "gains" if last else "sums", outs, scratch, 4.0,
                input_output_aliases={at: 0, at + 1: 1} if state else {},
            )(*sides, *rows, *state)
        return state

    left, counts, send, needed = one_round(first_round)

    def more_rounds():
        def step(state):
            turn, left, counts = state
            more_left, more_counts, _, _ = one_round(turn)
            return turn + 1, left + more_left, counts + more_counts

        _, all_left, all_counts = lax.while_loop(lambda state: state[0][0] < needed[0], step, (first_round + 1, left, counts))
        tallies = jnp.sum(all_counts, axis=1).reshape(features, BINS, 1)
        gains = gains_of(all_left.reshape(features, BINS, width), tallies).reshape(chips, lines, per_owner, BINS)
        last = jnp.arange(BINS) == BINS - 1
        gains = jnp.where(last, jnp.max(jnp.where(last, 0.0, gains)), gains)
        gains = jnp.stack([lax.dynamic_index_in_dim(gains, x ^ d, 0, keepdims=False) for d in range(chips)])
        line_of = [place // (groups_all // sets) % lines for place in range(groups_all)]
        rows = jnp.stack([gains[:, line].reshape(chips, 1, load) for line in line_of])
        return jnp.broadcast_to(rows, (groups_all, chips, 2, load)).reshape(send.shape)

    send = lax.cond(needed[0] > 1, more_rounds, lambda: send)
    got = lax.all_to_all(send, ("rows", "feat"), 0, 0)
    gains, best = kernel(
        functools.partial(finish_kernel, chips, slots, copies, lines, sets, groups_all), "finish",
        [shaped(jnp.float32, owned, BINS - 1), shaped(jnp.float32, 1, NODES)],
        [pltpu.VMEM((per_owner * NODES, BINS - 1), jnp.float32)],
    )(got)
    return gains, best.reshape(NODES)


def solution(mesh):
    in_specs = (P("rows", "feat"), P("feat", None), P(), P("rows", "feat"), P("rows"), P("rows"))
    out_specs = (P(("feat", "rows"), None), P())
    sizes = (mesh.shape["rows"], mesh.shape["feat"])
    return jax.shard_map(
        functools.partial(split_rows, sizes), mesh=mesh, in_specs=in_specs, out_specs=out_specs, check_vma=False
    )
```

```python
import functools
import math

import jax
import jax.numpy as jnp
from jax import lax
from jax.experimental import pallas as pl
from jax.experimental.pallas import tpu as pltpu
from jax.sharding import PartitionSpec as P

BINS = 32
NODES = 8
LANES = 128
CHUNKS = 4
EXTRA = 16
STEPS = 65536.0
PARAMS = pltpu.CompilerParams(vmem_limit_bytes=24 * 1024 * 1024)
VMEM = pl.BlockSpec(memory_space=pltpu.VMEM)
SMEM = pl.BlockSpec(memory_space=pltpu.SMEM)
HBM = pl.BlockSpec(memory_space=pltpu.HBM)
ANY = pl.BlockSpec(memory_space=pl.ANY)


def rank_of(node, live):
    groups = node.shape[0]
    block = groups * LANES
    members = [jnp.where((node == n) & live, 1.0, 0.0) for n in range(NODES)]
    member = jnp.concatenate(members, axis=0)
    size = NODES * groups
    i = lax.broadcasted_iota(jnp.int32, (LANES, LANES), 0)
    j = lax.broadcasted_iota(jnp.int32, (LANES, LANES), 1)
    before = jnp.where(i < j, 1.0, 0.0).astype(jnp.bfloat16)
    inside = jnp.dot(member.astype(jnp.bfloat16), before, preferred_element_type=jnp.float32)
    count = jnp.sum(member, axis=1, keepdims=True)
    p = lax.broadcasted_iota(jnp.int32, (size, size), 0)
    q = lax.broadcasted_iota(jnp.int32, (size, size), 1)
    earlier = jnp.where((p // groups == q // groups) & (q < p), 1.0, 0.0).astype(jnp.bfloat16)
    spread = jnp.broadcast_to(count, (size, LANES))
    base = jnp.dot(earlier, spread.astype(jnp.bfloat16), preferred_element_type=jnp.float32)
    rank = inside + base
    pos = jnp.zeros((groups, LANES), jnp.float32)
    for n in range(NODES):
        pos += members[n] * (rank[n * groups : (n + 1) * groups] + float(n * block))
    return jnp.where(live, pos, -1.0).astype(jnp.int32), jnp.max(base + spread).astype(jnp.int32)


def choose_rows(pos_ref, pick, distance, slots, room, x, a, turn):
    groups = pos_ref.shape[0]
    block = groups * LANES
    for slot in range(slots):
        node = (x ^ distance) * slots + (a ^ slot)
        wanted = lax.broadcasted_iota(jnp.int32, (room, LANES), 0) + turn * room + node * block
        for g in range(groups):
            pick[slot * room : (slot + 1) * room, g * LANES : (g + 1) * LANES] = jnp.where(
                pos_ref[g : g + 1, :] == wanted, 1.0, 0.0
            ).astype(jnp.bfloat16)


def moved(codes, pick):
    return lax.dot_general(codes, pick, (((1,), (1,)), ((), ())), preferred_element_type=jnp.float32)


def major_of(place, slots):
    copies = lax.axis_size("rows") // slots
    return place >> (copies.bit_length() - 1)


def theirs_kernel(targets_ref, theirs_ref, sems):
    copy_half(targets_ref, theirs_ref, sems, 1 - (lax.axis_index("feat") & 1))


def copy_half(targets_ref, out_ref, sems, half, between=None):
    block = out_ref.shape[0]
    piece = block // CHUNKS
    pieces = []
    for i in range(CHUNKS):
        source = targets_ref.at[pl.ds(pl.multiple_of(half * block + i * piece, piece), piece), :]
        pieces.append(pltpu.make_async_copy(source, out_ref.at[pl.ds(i * piece, piece), :], sems.at[i]))
    for copy in pieces:
        copy.start()
    if between:
        between()
    for copy in pieces:
        copy.wait()


def prepare_kernel(copies, codes_ref, give_ref, mine_ref):
    block = mine_ref.shape[1]
    part = codes_ref.shape[0] // copies
    core = lax.axis_index("feat") & 1
    minor = lax.axis_index("rows") & (copies - 1)
    for out_ref, half in ((give_ref, 1 - core), (mine_ref, core)):
        rows = pl.ds(pl.multiple_of(half * block, block), block)
        parts = [codes_ref[pl.ds((minor ^ d) * part, part), rows] for d in range(copies)]
        out_ref[...] = jnp.concatenate(parts, axis=0).astype(jnp.float32).astype(jnp.bfloat16)


def order_kernel(slots, room, turn_ref, targets_ref, node_ref, boot_ref, pos_ref, rounds_ref, own_ref, *refs):
    picks, sems = refs[:-1], refs[-1]
    feat, place = lax.axis_index("feat"), lax.axis_index("rows")

    def order():
        groups = pos_ref.shape[0]
        lines = pl.ds(pl.multiple_of((feat & 1) * groups, groups), groups)
        pos, most = rank_of(node_ref[lines, :], boot_ref[lines, :] > 0)
        pos_ref[...] = pos
        rounds_ref[...] = jnp.broadcast_to((most + (room - 1)) // room, rounds_ref.shape)
        for distance, pick in enumerate(picks, 1):
            choose_rows(pos_ref, pick, distance, slots, room, feat >> 1, major_of(place, slots), turn_ref[:1, :])

    copy_half(targets_ref, own_ref, sems, feat & 1, order)


def turns_of(pick, t0_ref, t1_ref, o0_ref, o1_ref):
    s0 = jnp.dot(pick, t0_ref[...], preferred_element_type=jnp.float32).astype(jnp.bfloat16)
    s1 = jnp.dot(pick, t1_ref[...], preferred_element_type=jnp.float32).astype(jnp.bfloat16)
    partial = jnp.dot(s0, o0_ref[...], preferred_element_type=jnp.float32)
    partial += jnp.dot(s1, o1_ref[...], preferred_element_type=jnp.float32)
    turns = partial * (0.5 / math.pi)
    return turns - jnp.floor(turns)


def send_kernel(first, rounds_ref, pick_ref, t0_ref, t1_ref, o0_ref, o1_ref, before_ref, out_ref, passed_ref):
    del before_ref
    passed_ref[...] = rounds_ref[...]
    turns = turns_of(pick_ref[first : first + out_ref.shape[0], :], t0_ref, t1_ref, o0_ref, o1_ref)
    out_ref[...] = (jnp.minimum((turns * STEPS).astype(jnp.int32), 65535) - 32768).astype(jnp.int16)


def codes_kernel(chips, copies, slots, room, turn_ref, rounds_ref, pos_ref, boot_ref, *refs):
    inputs, pick, outs = refs[:chips], refs[chips], refs[chips + 1 :]
    feat, place = lax.axis_index("feat"), lax.axis_index("rows")
    choose_rows(pos_ref, pick, 0, slots, room, feat >> 1, major_of(place, slots), turn_ref[:1, :])
    features, block = inputs[0].shape[0] // 2, inputs[0].shape[1]
    groups = block // LANES
    first = pl.multiple_of((lax.axis_index("feat") & 1) * groups, groups)
    weights = boot_ref[pl.ds(first, groups), :].astype(jnp.float32)
    row = lax.broadcasted_iota(jnp.int32, (EXTRA, LANES), 0)
    extra = [jnp.where(row == 0, weights[g : g + 1, :], 0.0) for g in range(groups)]
    extra = jnp.concatenate(extra, axis=1).astype(jnp.bfloat16)
    codes = jnp.concatenate([ref[...] for ref in inputs] + [extra], axis=0)
    own = moved(codes, pick[...])
    part = features // copies
    lines = []
    for d in range(copies):
        for core in range(2):
            lines += [own[(2 * chip + core) * features + d * part :][:part] for chip in range(chips)]
            if chips * part % EXTRA:
                lines.append(jnp.zeros((-chips * part % EXTRA, own.shape[1]), jnp.float32))
    last = own[2 * chips * features :]
    line = lax.broadcasted_iota(jnp.int32, last.shape, 0)
    lines.append(jnp.where(line == 1, rounds_ref[:1, :1].astype(jnp.float32), last))
    lines = jnp.concatenate(lines, axis=0).astype(jnp.bfloat16)
    for slot, out_ref in enumerate(outs):
        out_ref[...] = lines[:, slot * room : (slot + 1) * room]


def keep_kernel(pick_ref, t0_ref, t1_ref, o0_ref, o1_ref, out_ref):
    out_ref[...] = turns_of(pick_ref[...], t0_ref, t1_ref, o0_ref, o1_ref)


def cosine_kernel(chips, first, own_ref, phase_ref, *refs):
    received, outs = refs[: chips - 1], refs[chips - 1 :]
    width = phase_ref.shape[1]
    room = outs[0].shape[0]
    scaling = math.sqrt(2.0 / width)
    series = [(-1.0) ** (k + 1) * (2 * math.pi) ** (2 * k + 1) / math.factorial(2 * k + 1) for k in range(7)]
    shift = phase_ref[...] * (0.5 / math.pi)
    for slot, out_ref in enumerate(outs):
        turns = own_ref[(first + slot) * room : (first + slot + 1) * room, :] + shift
        for ref in received:
            turns += (ref[slot * room : (slot + 1) * room, :].astype(jnp.float32) + 32768.5) * (1.0 / STEPS)
        turns = jnp.abs(turns - jnp.floor(turns + 0.5)) - 0.25
        square = turns * turns
        value = jnp.full_like(turns, series[-1])
        for term in series[-2::-1]:
            value = value * square + term
        out_ref[...] = (scaling * (value * turns)).astype(jnp.bfloat16)


def far_cosine_kernel(chips, first, pinned, rounds_ref, own_ref, phase_ref, *refs):
    refs[-1][...] = rounds_ref[...]
    cosine_kernel(chips, first, own_ref, phase_ref, *refs[: chips - 1], *refs[chips - 1 + pinned : -1])


def parts_kernel(copies, *refs):
    pieces, outs = refs[:-2], refs[-2:]
    room = pieces[0].shape[1]
    lines = (pieces[0].shape[0] - EXTRA) // copies // 2
    each = lines + EXTRA
    for slot, piece in enumerate(pieces):
        span = slice(slot * room, (slot + 1) * room)
        for d in range(copies):
            for core, out_ref in enumerate(outs):
                at = (2 * d + core) * lines
                out_ref[d * each : d * each + lines, span] = piece[at : at + lines, :]
                out_ref[d * each + lines : (d + 1) * each, span] = piece[2 * copies * lines :, :]


def after_kernel(*refs):
    pass


def gains_of(left, counts):
    whole = left[..., BINS - 1 :, :]
    total = counts[..., BINS - 1 :, :]
    other = total - counts
    differ = left * (1.0 / jnp.maximum(counts, 1.0)) - (whole - left) * (1.0 / jnp.maximum(other, 1.0))
    return (counts * other / total) * jnp.sum(differ * differ, axis=-1, keepdims=True)


def add_rows(features, plan, parcels, pieces, earlier, left_ref, counts_ref, table):
    lines = -(-features // EXTRA) * EXTRA
    codes, weights = [], []
    for (index, at, first), piece in zip(plan, pieces):
        span = slice(first, first + piece.shape[0])
        codes.append(parcels[index][at : at + lines, span].astype(jnp.float32))
        weights.append(parcels[index][at + lines : at + lines + EXTRA, span].astype(jnp.float32)[:1])
    codes, weight = jnp.concatenate(codes, axis=1), jnp.concatenate(weights, axis=1)
    length = weight.shape[1]
    threshold = lax.broadcasted_iota(jnp.int32, (BINS, length), 0).astype(jnp.float32)
    for f in range(features):
        rows = slice(f * BINS, (f + 1) * BINS)
        entry = jnp.where(codes[f : f + 1, :] <= threshold, weight, 0.0)
        table[rows, :] = entry.astype(jnp.bfloat16)
        folded = entry[:, :LANES]
        for g in range(1, length // LANES):
            folded += entry[:, g * LANES : (g + 1) * LANES]
        counts_ref[rows, :] = earlier[1][rows, :] + folded if earlier else folded
    block = jnp.concatenate([piece[...] for piece in pieces], axis=0)
    sums = jnp.dot(table[...], block, preferred_element_type=jnp.float32)
    left_ref[...] = earlier[0][...] + sums if earlier else sums


def sums_kernel(features, plan, parcels, *refs):
    pieces, earlier = refs[parcels : parcels + len(plan)], refs[parcels + len(plan) : -3]
    add_rows(features, plan, refs[:parcels], pieces, earlier, *refs[-3:])


def gains_kernel(features, plan, parcels, lines, sets, groups, chips, *refs):
    send_ref, needed_ref, left_ref, counts_ref, table = refs[-5:]
    sums_kernel(features, plan, parcels, *refs[:-5], left_ref, counts_ref, table)
    needed = 0.0
    for parcel in refs[:parcels]:
        for at in range(0, parcel.shape[0], EXTRA):
            if (at + EXTRA) % (-(-features // EXTRA) * EXTRA + EXTRA) == 0:
                flags = parcel[at : at + EXTRA, :].astype(jnp.float32)
                line = lax.broadcasted_iota(jnp.int32, flags.shape, 0)
                needed = jnp.maximum(needed, jnp.max(jnp.where(line == 1, flags, 0.0)))
    needed_ref[0] = needed.astype(jnp.int32)
    x = lax.axis_index("feat") >> 1
    columns = []
    largest = jnp.zeros((1, 1), jnp.float32)
    threshold = lax.broadcasted_iota(jnp.int32, (BINS, 1), 0)
    for f in range(features):
        rows = slice(f * BINS, (f + 1) * BINS)
        counts = jnp.sum(counts_ref[rows, :], axis=1, keepdims=True)
        column = gains_of(left_ref[rows, :], counts)
        column = jnp.where(threshold < BINS - 1, column, 0.0)
        largest = jnp.maximum(largest, jnp.max(column, axis=0, keepdims=True))
        columns.append(column)
    load = send_ref.shape[2]
    wide = load // BINS
    fill = jnp.broadcast_to(largest, (BINS, 1))
    i = lax.broadcasted_iota(jnp.int32, (load, load), 0)
    j = lax.broadcasted_iota(jnp.int32, (load, load), 1)
    for d in range(chips):
        for line in range(lines):
            first = (d * lines + line) * wide
            column = jnp.concatenate([jnp.where(threshold < BINS - 1, c, fill) for c in columns[first : first + wide]], axis=0)
            row = jnp.sum(jnp.where(i == j, column, 0.0), axis=0, keepdims=True)
            for place in range(groups):
                if place // (groups // sets) % lines == line:
                    for core in range(2):
                        send_ref[place * 2 * chips + 2 * (x ^ d) + core] = row


def finish_kernel(chips, slots, copies, lines, sets, groups, got_ref, gains_ref, best_ref, rows_ref):
    feat, place = lax.axis_index("feat"), lax.axis_index("rows")
    core = feat & 1
    per_set = groups // sets
    source = (place >> (per_set.bit_length() - 1)) >> (lines.bit_length() - 1)
    load = got_ref.shape[2]
    own, top = [], []
    for node in range(NODES):
        x, a = node // slots, node % slots
        index = lambda b, c: (a * copies + b) * 2 * chips + 2 * x + c
        own.append(got_ref[index(source, core)])
        largest = got_ref[index(0, 0)]
        for b in range(copies):
            for c in range(2):
                largest = jnp.maximum(largest, got_ref[index(b, c)])
        top.append(largest)
    own, top = jnp.concatenate(own, axis=0), jnp.concatenate(top, axis=0)
    for f in range(load // BINS):
        rows_ref[f * NODES : (f + 1) * NODES, :] = own[:, f * BINS : (f + 1) * BINS - 1]
    owned = gains_ref.shape[0]
    first = (place * owned) & (rows_ref.shape[0] - 1)
    gains_ref[...] = rows_ref[pl.ds(first, owned), :]
    i = lax.broadcasted_iota(jnp.int32, (NODES, NODES), 0)
    j = lax.broadcasted_iota(jnp.int32, (NODES, NODES), 1)
    best_ref[...] = jnp.sum(jnp.where(i == j, top[:, BINS - 1 : BINS], 0.0), axis=0, keepdims=True)


def split_rows(mesh_sizes, targets, omega, phase, codes, node, boot_counts):
    groups_all, feat_all = mesh_sizes
    chips = feat_all // 2
    slots = NODES // chips
    copies = groups_all // slots
    rows_dev, feat_dev = codes.shape
    width = omega.shape[1]
    block = rows_dev // 2
    room = block // NODES
    owned = feat_dev * NODES // groups_all
    per_owner = max(1, owned // NODES)
    sets = feat_dev // per_owner
    lines = sets // copies
    part = lines * per_owner
    features = chips * part

    feat = lax.axis_index("feat")
    x = feat // 2
    span = slots * room
    load = per_owner * BINS
    columns = targets.shape[1]

    def permute(axis, size, distance, array):
        return lax.ppermute(array, axis, [(i, i ^ distance) for i in range(size)])

    swap = functools.partial(permute, "feat", feat_all, 1)

    def along_x(distance, array):
        return permute("feat", feat_all, 2 * distance, array)

    def along_major(distance, array):
        return permute("rows", groups_all, copies * distance, array)

    def along_minor(distance, array):
        return permute("rows", groups_all, distance, array)

    def shaped(kind, *shape):
        return jax.ShapeDtypeStruct(shape, kind)

    def kernel(body, name, outs, scratch=(), micros=0.3, hbm=(), **more):
        def call(*arrays):
            ins = [SMEM if a.shape == (1,) else HBM if i in hbm else VMEM for i, a in enumerate(arrays)]
            return pl.pallas_call(
                body, out_shape=tuple(outs), in_specs=ins, scratch_shapes=list(scratch), compiler_params=PARAMS, name=name,
                out_specs=tuple(SMEM if out.shape == (1,) else VMEM for out in outs),
                cost_estimate=pl.CostEstimate(flops=int(micros * 1e9), bytes_accessed=1 << 16, transcendentals=0), **more,
            )(*arrays)

        return call

    first_round = jnp.zeros((8, LANES), jnp.int32)
    node_lines = node.reshape(rows_dev // LANES, LANES)
    boot_lines = boot_counts.reshape(rows_dev // LANES, LANES)
    token = shaped(jnp.int32, 8, LANES)
    def after(array, *others):
        return pl.pallas_call(
            after_kernel, out_shape=shaped(array.dtype, *array.shape), in_specs=[ANY] * (1 + len(others)), out_specs=ANY,
            input_output_aliases={0: 0}, compiler_params=PARAMS, name="after",
        )(array, *others)

    half = shaped(jnp.bfloat16, block, columns)
    sems = [pltpu.SemaphoreType.DMA((CHUNKS,))]
    (theirs,) = kernel(theirs_kernel, "theirs", [half], sems, hbm=(0,))(targets)
    theirs, omega_theirs = swap(theirs), swap(omega)
    def order(turn):
        outs = [shaped(jnp.int32, block // LANES, LANES), token, half] + [shaped(jnp.bfloat16, span, block)] * (chips - 1)
        return kernel(functools.partial(order_kernel, slots, room), "order", outs, sems, hbm=(1,))(
            turn, targets, node_lines, boot_lines
        )

    first_order = order(first_round)
    give, mine = kernel(
        functools.partial(prepare_kernel, copies), "prepare", [shaped(jnp.bfloat16, feat_dev, block)] * 2
    )(codes.T)
    halves = [jnp.concatenate([mine, swap(give)], axis=0)]
    halves += [along_x(d, halves[0]) for d in range(1, chips)]
    lines_part = -(-features // EXTRA) * EXTRA
    lines_all = 2 * copies * lines_part + EXTRA
    each = lines_part + EXTRA
    line = phase.reshape(1, width)
    near = slots // 2
    parts = [(0, near), (near, slots - near)]

    def one_round(turn, ordered, more):
        pos, rounds, own, *picks = ordered
        operands = (own, theirs, omega, omega_theirs)
        angles = {}
        for first, count in parts[::-1]:
            received = []
            for d in range(1, chips):
                sent, rounds = kernel(
                    functools.partial(send_kernel, first * room), "send",
                    [shaped(jnp.int16, count * room, width), token], micros=0.05,
                )(rounds, picks[d - 1], *operands, halves[0])
                received.append(along_x(d, sent))
            angles[first] = received
        pick, *pieces = kernel(
            functools.partial(codes_kernel, chips, copies, slots, room), "codes",
            [shaped(jnp.bfloat16, span, block)] + [shaped(jnp.bfloat16, lines_all, room)] * slots, micros=0.05,
        )(turn, rounds, pos, boot_lines, *halves)
        pieces = [along_major(d, pieces[d]) if d else pieces[d] for d in range(slots)]
        (own_angles,) = kernel(keep_kernel, "keep", [shaped(jnp.float32, span, width)], micros=4.0)(pick, *operands)
        pinned = pieces[1:-1]
        *far, rounds = kernel(
            functools.partial(far_cosine_kernel, chips, near, len(pinned)), "cosine_far",
            [shaped(jnp.bfloat16, room, width)] * (slots - near) + [token],
        )(rounds, own_angles, line, *angles[near], *pinned)
        stay, cross = kernel(
            functools.partial(parts_kernel, copies), "parts", [shaped(jnp.bfloat16, copies * each, span)] * 2
        )(*pieces)
        far = [along_major(near + i, f) for i, f in enumerate(far)]
        come = swap(cross)
        close = kernel(
            functools.partial(cosine_kernel, chips, 0), "cosine_near", [shaped(jnp.bfloat16, room, width)] * near
        )(own_angles, line, *angles[0])
        close = [along_major(d, f) if d else f for d, f in enumerate(close)]
        parcels = [stay[:each], come[:each]]
        for d in range(1, copies):
            both = jnp.concatenate([stay[d * each : (d + 1) * each], come[d * each : (d + 1) * each]], axis=0)
            parcels.append(along_minor(d, both))
        late = []
        for first, group in ((0, close), (near * room, far)):
            rows = jnp.concatenate(group, axis=0)
            if first:
                rows = after(rows, *parcels[2:])
            for d in range(copies):
                piece = along_minor(d, rows) if d else rows
                late += [((d and d + 1, 0, first), piece), ((d + 1, d and each, first), swap(piece))]
        sums = [shaped(jnp.float32, features * BINS, width), shaped(jnp.float32, features * BINS, LANES)]
        table = pltpu.VMEM((features * BINS, 2 * copies * (slots - near) * room), jnp.bfloat16)
        state = []
        for items in (late[: 2 * copies], late[2 * copies :]):
            plan, pieces = [item[0] for item in items], [item[1] for item in items]
            if state and not more:
                body = functools.partial(gains_kernel, features, plan, len(parcels), lines, sets, groups_all, chips)
                outs = [shaped(jnp.float32, groups_all * feat_all, 1, load), shaped(jnp.int32, 1)]
                scratch = [pltpu.VMEM(a.shape, a.dtype) for a in sums] + [table]
                return kernel(body, "gains", outs, scratch)(*parcels, *pieces, *state)
            state = kernel(functools.partial(sums_kernel, features, plan, len(parcels)), "sums", sums, [table])(
                *parcels, *pieces, *state
            )
        return state

    send, needed = one_round(first_round, first_order, False)

    def more_rounds():
        def step(state):
            turn, left, counts = state
            more_left, more_counts = one_round(turn, order(turn), True)
            return turn + 1, left + more_left, counts + more_counts

        zeros = [jnp.zeros((features * BINS, n), jnp.float32) for n in (width, LANES)]
        _, all_left, all_counts = lax.while_loop(lambda state: state[0][0, 0] < needed[0], step, (first_round, *zeros))
        tallies = jnp.sum(all_counts, axis=1).reshape(features, BINS, 1)
        gains = gains_of(all_left.reshape(features, BINS, width), tallies).reshape(chips, lines, per_owner, BINS)
        last = jnp.arange(BINS) == BINS - 1
        gains = jnp.where(last, jnp.max(jnp.where(last, 0.0, gains)), gains)
        gains = jnp.stack([lax.dynamic_index_in_dim(gains, x ^ d, 0, keepdims=False) for d in range(chips)])
        line_of = [place // (groups_all // sets) % lines for place in range(groups_all)]
        rows = jnp.stack([gains[:, line].reshape(chips, 1, load) for line in line_of])
        return jnp.broadcast_to(rows, (groups_all, chips, 2, load)).reshape(send.shape)

    send = lax.cond(needed[0] > 1, more_rounds, lambda: send)
    got = lax.all_to_all(send, ("rows", "feat"), 0, 0)
    gains, best = kernel(
        functools.partial(finish_kernel, chips, slots, copies, lines, sets, groups_all), "finish",
        [shaped(jnp.float32, owned, BINS - 1), shaped(jnp.float32, 1, NODES)],
        [pltpu.VMEM((per_owner * NODES, BINS - 1), jnp.float32)],
    )(got)
    return gains, best.reshape(NODES)


def solution(mesh):
    in_specs = (P("rows", "feat"), P("feat", None), P(), P("rows", "feat"), P("rows"), P("rows"))
    out_specs = (P(("feat", "rows"), None), P())
    sizes = (mesh.shape["rows"], mesh.shape["feat"])
    return jax.shard_map(
        functools.partial(split_rows, sizes), mesh=mesh, in_specs=in_specs, out_specs=out_specs, check_vma=False
    )
```
